32 devices in a mesh: row: 4 (over z), col: 8 (over y, x, core).
Axes of the slice: x: 2, y: 2, z: 4, core: 2. Of those that a mesh axis runs over, the one named last changes fastest.
Arguments:
- ancestor: float32 [24576, 24576], P('row', 'col'), may hold values from -6 to 6
- lhat_one: float32 [24576, 512], P('col', 'row'), may hold values from -0.109375 to 0.109375
- lhat_two: float32 [24576, 512], P('col', 'row'), may hold values from -0.109375 to 0.109375
- link_two: float32 [512, 512], replicated, may hold values from -0.25 to 0.25
- diag_one: float32 [512, 512], replicated, may hold values from -6 to 6
- diag_two: float32 [512, 512], replicated, may hold values from -6 to 6
- mask_one: int32 [192], replicated, may hold values from 0 to 1, as said below
- mask_two: int32 [192], replicated, may hold values from 0 to 1, as said below
Outputs:
- x_one: float32 [24576, 512], P('row', 'col')
- d_one: float32 [512, 512], replicated
- x_two: float32 [24576, 512], P('row', 'col')
- link_inverse: float32 [512, 512], replicated
- d_two: float32 [512, 512], replicated
The draws below stay inside these ranges and needn't reach their ends.
Inputs may be any that keep to these rules, and one draw needn't show every extreme that they name: `mask_one`: 1 where a block of 128 factor rows is nonzero, else 0; the last block is always nonzero. `mask_two`: 1 where a block of 128 factor rows is nonzero, else 0; the last block is always nonzero.
All inputs are finite; a program needn't handle non-finite values.
Results may differ from the reference program's by a relative error of at most 0.00011.
Values sent between devices are 32-bit elements; how exact they have to be, the bound alone decides.
A program may use at most 192 MiB of HBM per device.

```python
import jax
import jax.numpy as jnp
from jax import lax

NA = 24576
W = 512
BLOCK = 128
NB = 192
N_COL = 8


def skewed_mask(key):
    position = jnp.arange(NB, dtype=jnp.int32)
    threshold = 150 + 850 * position // max(NB - 1, 1)
    drawn = jax.random.randint(key, (NB,), 0, 1000, dtype=jnp.int32)
    return (drawn < threshold).astype(jnp.int32)


def draw_mask_one(key, part):
    return skewed_mask(jax.random.fold_in(key, 11))


def draw_mask_two(key, part):
    return skewed_mask(jax.random.fold_in(key, 23))


def steps_of(stream_key, dims, split, least, top_value):
    level, own = 1.0, jax.random.fold_in(stream_key, 6)
    for dim, parts in split:
        steps = jnp.exp(jax.random.uniform(jax.random.fold_in(own, dim), (parts,), jnp.float32, least / len(split), top_value / len(split)))
        level = level * jnp.repeat(steps, dims[dim] // parts).reshape([-1 if axis == dim else 1 for axis in range(len(dims))])
    return level


def gaussian(own_key, extent, deviation, limit, split=(), kind=jnp.bfloat16):
    array = jax.random.normal(own_key, extent, jnp.float32) * deviation
    if len(split) > 0:
        array = steps_of(own_key, extent, split, -0.22, 0.18) * array
    return jnp.clip(array, min=-limit, max=limit).astype(kind)


def setup_inputs(seed: int = 0) -> dict:
    key_list = jax.random.split(jax.random.key(seed), 9)
    ancestor = gaussian(key_list[0], (NA, NA), 1.0, 6.0, ((0, 4), (1, 8)), jnp.float32)
    lhat_one = gaussian(key_list[1], (NA, W), (NA // N_COL) ** -0.5, 0.109375, ((0, 8), (1, 4)), jnp.float32)
    lhat_two = gaussian(key_list[2], (NA, W), (NA // N_COL) ** -0.5, 0.109375, ((0, 8), (1, 4)), jnp.float32)
    link_two = gaussian(key_list[3], (W, W), W ** -0.5, 0.25, (), jnp.float32)
    diag_one = gaussian(key_list[4], (W, W), 1.0, 6.0, (), jnp.float32)
    diag_two = gaussian(key_list[5], (W, W), 1.0, 6.0, (), jnp.float32)
    mask_one = draw_mask_one(jax.random.fold_in(key_list[8], 71), 0)
    mask_two = draw_mask_two(jax.random.fold_in(key_list[8], 71), 0)
    return dict(ancestor=ancestor, lhat_one=lhat_one, lhat_two=lhat_two, link_two=link_two, diag_one=diag_one, diag_two=diag_two, mask_one=mask_one, mask_two=mask_two)


def masked(factor_rows, block_mask):
    expanded = jnp.repeat(block_mask.astype(jnp.float32), BLOCK, total_repeat_length=NA)
    return factor_rows * expanded[:, None]


def product(left, right):
    return jnp.dot(left, right, precision=lax.Precision.HIGHEST, preferred_element_type=jnp.float32)


def reference(ancestor, lhat_one, lhat_two, link_two, diag_one, diag_two, mask_one, mask_two):
    factor_one = masked(lhat_one, mask_one)
    factor_two = masked(lhat_two, mask_two)
    x_one = -product(ancestor, factor_one)
    d_one = diag_one - product(factor_one.T, x_one)
    x_two = -(product(ancestor, factor_two) + product(x_one, link_two))
    link_inverse = -(product(x_one.T, factor_two) + product(d_one, link_two))
    d_two = diag_two - product(factor_two.T, x_two) - product(link_two.T, link_inverse)
    return x_one, d_one, x_two, link_inverse, d_two
```

```python
import functools

import jax
import jax.numpy as jnp
from jax import lax
from jax.experimental import pallas as pl
from jax.experimental.pallas import tpu as pltpu
from jax.sharding import PartitionSpec as P

BLOCK = 128
PIECES = 2
NT = (((1,), (1,)), ((), ()))


def product(left, right):
    return jnp.dot(left, right, precision=lax.Precision.HIGHEST, preferred_element_type=jnp.float32)


def product_nt(left, right):
    return lax.dot_general(
        left, right, NT, precision=lax.Precision.HIGHEST, preferred_element_type=jnp.float32
    )


def halves(value):
    high = value.astype(jnp.bfloat16)
    low = (value - high.astype(jnp.float32)).astype(jnp.bfloat16)
    return high, low


def ancestor_kernel(factor_ref, ancestor_ref, out_ref, high_ref, low_ref):
    @pl.when(pl.program_id(0) == 0)
    def _():
        high, low = halves(factor_ref[...])
        high_ref[...] = high
        low_ref[...] = low

    left_high, left_low = halves(ancestor_ref[...])
    dot = functools.partial(
        lax.dot_general, dimension_numbers=NT, preferred_element_type=jnp.float32
    )
    total = dot(left_high, low_ref[...]) + dot(left_low, high_ref[...])
    total = total + dot(left_high, high_ref[...])
    out_ref[...] = total.T


def ancestor_product(factor, ancestor):
    wide, depth = factor.shape
    rows = ancestor.shape[0]
    tile = min(512, rows)
    return pl.pallas_call(
        ancestor_kernel,
        grid=(rows // tile,),
        out_shape=jax.ShapeDtypeStruct((wide, rows), jnp.float32),
        in_specs=[
            pl.BlockSpec((wide, depth), lambda i: (0, 0)),
            pl.BlockSpec((tile, depth), lambda i: (i, 0)),
        ],
        out_specs=pl.BlockSpec((wide, tile), lambda i: (0, i)),
        scratch_shapes=[pltpu.VMEM((wide, depth), jnp.bfloat16)] * 2,
        compiler_params=pltpu.CompilerParams(vmem_limit_bytes=48 * 1024 * 1024),
        cost_estimate=pl.CostEstimate(
            flops=6 * wide * depth * rows,
            bytes_accessed=4 * (rows * depth + wide * depth + wide * rows),
            transcendentals=0,
        ),
    )(factor, ancestor)


def per_device(ancestor, lhat_one, lhat_two, link_two, diag_one, diag_two, mask_one, mask_two):
    column_index = lax.axis_index("col")
    row_count = lax.axis_size("row")
    column_count = lax.axis_size("col")
    column_rows = lhat_one.shape[0]
    ancestor_rows = ancestor.shape[0]
    full_width = link_two.shape[0]
    own_width = full_width // column_count
    piece = own_width // PIECES
    share = piece // row_count
    blocks = column_rows // BLOCK
    bits = column_count.bit_length() - 1

    def factor(factor_part, block_mask):
        mask_part = lax.dynamic_slice_in_dim(block_mask, column_index * blocks, blocks)
        expanded = jnp.repeat(-mask_part.astype(jnp.float32), BLOCK, total_repeat_length=column_rows)
        part = (factor_part * expanded[:, None]).T
        part = part.reshape(-1, PIECES, piece, column_rows)
        return [
            lax.all_gather(part[:, q], "row", axis=0, tiled=True).reshape(-1, column_rows)
            for q in range(PIECES)
        ]

    def exchange(value, order, remaining):
        for bit in order:
            axis = remaining.index(bit)
            remaining = remaining[:axis] + remaining[axis + 1:]
            mine = (column_index >> bit) & 1
            outgoing = lax.dynamic_index_in_dim(value, 1 - mine, axis, keepdims=False)
            kept = lax.dynamic_index_in_dim(value, mine, axis, keepdims=False)
            pairs = [(i, i ^ (1 << bit)) for i in range(column_count)]
            value = kept + lax.ppermute(outgoing, "col", pairs)
        return value, remaining

    def row_sum(partial_value):
        value = partial_value.reshape((2,) * bits + (piece, ancestor_rows))
        value, remaining = exchange(value, (0,), tuple(reversed(range(bits))))
        upper, lower = value[..., : piece // 2, :], value[..., piece // 2:, :]
        upward = tuple(range(1, bits))
        upper, _ = exchange(upper, upward, remaining)
        lower, _ = exchange(lower, upward[::-1], remaining)
        return jnp.concatenate([upper, lower], axis=0)

    def mirror(own):
        outgoing = own.reshape(row_count, share, ancestor_rows)
        arrived = lax.all_to_all(outgoing, "row", split_axis=0, concat_axis=0, tiled=True)
        spread = arrived.reshape(row_count, share, column_count // row_count, column_rows)
        spread = spread.transpose(0, 2, 1, 3).reshape(column_count, share, column_rows)
        landed = lax.all_to_all(spread, "col", split_axis=0, concat_axis=0, tiled=True)
        return landed.reshape(column_count * share, column_rows)

    def device_sum(partial_value):
        width = partial_value.shape[1]
        outgoing = partial_value.reshape(column_count, -1, width)
        arrived = lax.all_to_all(outgoing, "col", split_axis=0, concat_axis=0, tiled=True)
        mine = jnp.sum(arrived, axis=0)
        complete = lax.all_gather(mine, ("row", "col"), axis=0, tiled=True)
        complete = complete.reshape(row_count, PIECES, column_count, share, -1, PIECES, column_count, piece)
        complete = complete.transpose(4, 2, 1, 0, 3, 6, 5, 7)
        return complete.reshape(-1, full_width, full_width)

    link_ordered = link_two.reshape(column_count, PIECES, piece, full_width)
    link_ordered = link_ordered.transpose(1, 0, 2, 3).reshape(full_width, full_width)
    link_columns = link_ordered.T.reshape(column_count, PIECES, piece, full_width)

    pieces_one = factor(lhat_one, mask_one)
    pieces_two = factor(lhat_two, mask_two)
    own_one = [row_sum(ancestor_product(part, ancestor)) for part in pieces_one]
    minus_one = jnp.concatenate(pieces_one, axis=0)
    own_two = []
    for q in range(PIECES):
        columns = link_columns[:, q].reshape(-1, full_width)
        combined = pieces_two[q] - product(columns, minus_one)
        own_two.append(row_sum(ancestor_product(combined, ancestor)))
    minus_two = jnp.concatenate(pieces_two, axis=0)

    mirrored_one = jnp.concatenate([mirror(own) for own in own_one], axis=0)
    first = jnp.concatenate(
        [product_nt(mirrored_one, minus_one), product_nt(mirrored_one, minus_two)], axis=1
    )
    diag_part, link_part = device_sum(first)
    d_one = diag_one + diag_part.T
    link_inverse = link_part - product(d_one, link_two)
    base_two = diag_two - product(link_two.T, link_inverse)

    last = jnp.concatenate([product_nt(mirror(own), minus_two) for own in own_two], axis=0)
    d_two = base_two + device_sum(last)[0].T
    x_one = jnp.concatenate(own_one, axis=0).T
    x_two = jnp.concatenate(own_two, axis=0).T
    return (x_one, d_one, x_two, link_inverse, d_two)


def solution(mesh):
    in_specs = (P("row", "col"), P("col", "row"), P("col", "row"), P(), P(), P(), P(), P())
    out_specs = (P("row", "col"), P(), P("row", "col"), P(), P())
    return jax.shard_map(
        per_device, mesh=mesh, in_specs=in_specs, out_specs=out_specs, check_vma=False
    )
```
